512 devices in a mesh: row: 16 (over y, z_hi, core), col: 32 (over z_lo, x).
Axes of the slice: x: 4, y: 4, z: 16 (z_hi: 2, z_lo: 8; z = z_hi * 8 + z_lo), core: 2. Of those that a mesh axis runs over, the one named last changes fastest.
Arguments:
- blocks: bfloat16 [16, 32, 128, 128, 128], P('row', 'col'), may hold values from -0.115722656 to 0.115722656
- block_rows: int32 [16, 32, 128], P('row', 'col'), may hold values from 0 to 31
- block_cols: int32 [16, 32, 128], P('row', 'col'), may hold values from 0 to 63
- counts: int32 [16, 32], P('row', 'col'), may hold values from 1 to 128, as said below
- sketch: bfloat16 [1024, 48, 128], P(('row', 'col')), may hold values from -6 to 6
- adjoint_sketch: bfloat16 [1024, 48, 128], P(('col', 'row')), may hold values from -6 to 6
Outputs:
- image: float32 [1024, 48, 128], P(('col', 'row'))
- coimage: float32 [1024, 48, 128], P(('row', 'col'))
The draws below stay inside these ranges and needn't reach their ends.
Inputs may be any that keep to these rules, and one draw needn't show every extreme that they name: `counts`: every draw has some tile with exactly 128 live slots; loads are skewed, the busiest some three times the mean.
All inputs are finite; a program needn't handle non-finite values.
Results may differ from the reference program's by a relative error of at most 0.0003.
Values may be sent and summed in bfloat16 or wider, within the bound.
A program may use at most 64 MiB of HBM per device.

```python
import jax
import jax.numpy as jnp
from jax import lax

BLK = 128
COLS = 48
SB = 2
K_MAX = 128
NR = 32
NC = 64
NBLK = 1024
N_ROW = 16
N_COL = 32


def draw_counts(key, part):
    key = jax.random.fold_in(key, 11)
    first, second = jax.random.split(key)
    base = jax.random.randint(first, (N_ROW * N_COL,), 1, K_MAX + 1)
    skewed = (base * base + K_MAX - 1) // K_MAX
    where = jax.random.randint(second, (), 0, N_ROW * N_COL)
    skewed = skewed.at[where].set(K_MAX)
    return skewed.reshape(N_ROW, N_COL).astype(jnp.int32)


def place_ends(values, key, least, high):
    place = [jax.random.randint(jax.random.fold_in(key, axis), (), 0, length) for axis, length in enumerate(values.shape)]
    widest = values.shape.index(max(values.shape))
    next_to = place[:widest] + [(place[widest] + 1) % values.shape[widest]] + place[widest + 1:]
    return values.at[tuple(place)].set(least).at[tuple(next_to)].set(high)


def block_scale(rng, dims, cuts, low, high):
    factor_of = 1.0
    for dim, blocks in cuts:
        steps = jax.random.uniform(jax.random.fold_in(jax.random.fold_in(rng, 6), dim), (blocks,), jnp.float32, low / len(cuts), high / len(cuts))
        factor_of = factor_of * jnp.repeat(jnp.exp(steps), dims[dim] // blocks).reshape((-1,) + (1,) * (len(dims) - 1 - dim))
    return factor_of


def bell_draw(own_key, extent, width, most, pieces=(), kind=jnp.bfloat16):
    values = jax.random.normal(own_key, extent, jnp.float32) * width
    if len(pieces) > 0:
        values = block_scale(own_key, extent, pieces, -0.22, 0.18) * values
    return jnp.clip(values, min=-most, max=most).astype(kind)


def setup_inputs(seed: int = 0) -> dict:
    keys = jax.random.split(jax.random.key(seed), 7)
    return {
        "blocks": bell_draw(keys[0], (N_ROW, N_COL, K_MAX, BLK, BLK), ((BLK * max(1, K_MAX // (3 * SB))) ** -0.5), 0.115722656, ((0, 16), (1, 32))),
        "block_rows": place_ends(jax.random.randint(keys[1], (N_ROW, N_COL, K_MAX), 0, NR), jax.random.fold_in(keys[1], 1), 0, NR - 1).astype(jnp.int32),
        "block_cols": place_ends(jax.random.randint(keys[2], (N_ROW, N_COL, K_MAX), 0, NC), jax.random.fold_in(keys[2], 1), 0, NC - 1).astype(jnp.int32),
        "counts": draw_counts(jax.random.fold_in(keys[6], 71), 0),
        "sketch": bell_draw(keys[4], (NBLK, COLS, BLK), 1.0, 6.0, ((0, 512),)),
        "adjoint_sketch": bell_draw(keys[5], (NBLK, COLS, BLK), 1.0, 6.0, ((0, 512),)),
    }


def reference(blocks, block_rows, block_cols, counts, sketch, adjoint_sketch):
    sketch_f = sketch.astype(jnp.float32)
    adjoint_f = adjoint_sketch.astype(jnp.float32)
    slot_ids = jnp.arange(K_MAX, dtype=jnp.int32)

    def per_tile(carry, inputs):
        image_acc, coimage_acc = carry
        tile, rows_k, cols_k, live_count, r_idx, c_idx = inputs
        tile_f = tile.astype(jnp.float32)
        global_rows = (c_idx * NR + rows_k).astype(jnp.int32)
        global_cols = (r_idx * NC + cols_k).astype(jnp.int32)
        weight = (slot_ids < live_count).astype(jnp.float32)
        taken = sketch_f[global_cols]
        forward = jnp.einsum("kab,kcb->kca", tile_f, taken) * weight[:, None, None]
        image_acc = image_acc.at[global_rows].add(forward)
        given = adjoint_f[global_rows]
        backward = jnp.einsum("kab,kca->kcb", tile_f, given) * weight[:, None, None]
        coimage_acc = coimage_acc.at[global_cols].add(backward)
        return (image_acc, coimage_acc), None

    r_grid = jnp.repeat(jnp.arange(N_ROW, dtype=jnp.int32), N_COL)
    c_grid = jnp.tile(jnp.arange(N_COL, dtype=jnp.int32), N_ROW)
    tiles = N_ROW * N_COL
    init = (jnp.zeros((NBLK, COLS, BLK), jnp.float32), jnp.zeros((NBLK, COLS, BLK), jnp.float32))
    (image, coimage), unused = lax.scan(per_tile, init, (blocks.reshape(tiles, K_MAX, BLK, BLK), block_rows.reshape(tiles, K_MAX), block_cols.reshape(tiles, K_MAX), counts.reshape(tiles), r_grid, c_grid))
    return image, coimage
```

```python
import jax
import jax.numpy as jnp
from jax import lax
from jax.experimental import pallas as pl
from jax.experimental.pallas import tpu as pltpu
from jax.sharding import PartitionSpec as P

SLOTS = 128
COLS = 48
BLK = 128
NR = 32
NC = 64
T_ROW, T_COL, T_PREVR, T_PREVC, T_LASTR, T_LASTC, T_END = 0, 128, 256, 384, 512, 576, 640
XS = (1, 3, 2)
Z_NEAR = (1, 2, 3, 4, 5, 6, 7)
Z_FAR = (7, 6, 5, 4, 3, 2, 1)
NSEM = 128


def kernel(tab, blk_hbm, sk_hbm, ad_hbm, img_ref, coi_ref,
           w, ga, gs, accr, accc, sx, rx, sz, rz, sc, rc, sy, ry, sh, rh,
           lsem, wsem, ssem, rsem):
    r = lax.axis_index("row")
    c = lax.axis_index("col")
    y, zh, co = r // 4, (r // 2) % 2, r % 2
    zl, x = c // 4, c % 4

    def flip(v, m):
        out = 0
        bit = 1
        while bit < 8:
            b = (v // bit) % 2
            out = out + bit * ((1 - b) if (m & bit) else b)
            bit *= 2
        return out

    def peer(my=0, mzh=0, mco=0, mz=0, mx=0):
        y2, zh2, co2 = flip(y, my), flip(zh, mzh), flip(co, mco)
        zl2, x2 = flip(zl, mz), flip(x, mx)
        return (y2 * 4 + zh2 * 2 + co2, zl2 * 4 + x2)

    peers = ([dict(mzh=1), dict(mco=1)] + [dict(mz=m) for m in Z_FAR]
             + [dict(mx=m) for m in XS] + [dict(my=m) for m in XS])
    bar = pltpu.get_barrier_semaphore()
    for p in peers:
        pl.semaphore_signal(bar, inc=1, device_id=peer(**p), device_id_type=pl.DeviceIdType.MESH)

    parts = 4
    loads = []
    for i in range(parts):
        n = SLOTS // parts
        cp = pltpu.make_async_copy(blk_hbm.at[0, 0, pl.ds(i * n, n)], w.at[pl.ds(i * n, n)], wsem.at[i])
        cp.start()
        loads.append(cp)

    def ga_at(y_, zh_, co_, n=2):
        return pl.ds((co_ * 8 + y_ * 2 + zh_) * 2, n)

    def gs_at(zl_, x_):
        return pl.ds((zl_ * 4 + x_) * 2, 2)

    own_ad = pltpu.make_async_copy(ad_hbm, ga.at[ga_at(y, zh, co)], lsem.at[0])
    own_sk = pltpu.make_async_copy(sk_hbm, gs.at[gs_at(zl, x)], lsem.at[1])
    own_ad.start()
    own_sk.start()
    accr[0] = jnp.zeros((COLS, BLK), jnp.float32)
    accc[0] = jnp.zeros((COLS, BLK), jnp.float32)
    pl.semaphore_wait(bar, len(peers))

    count = [0]
    sent = []

    def send(src, dst, **p):
        i = count[0]
        count[0] += 1
        cp = pltpu.make_async_remote_copy(
            src_ref=src, dst_ref=dst, send_sem=ssem.at[i], recv_sem=rsem.at[i],
            device_id=peer(**p), device_id_type=pl.DeviceIdType.MESH)
        cp.start()
        sent.append(cp)
        return cp

    own_ga, own_gs = ga.at[ga_at(y, zh, co)], gs.at[gs_at(zl, x)]
    a_zh = send(ad_hbm, own_ga, mzh=1)
    s_z = {m: send(sk_hbm, own_gs, mz=m) for m in Z_FAR}
    a_y = {(m, 0): send(ad_hbm, own_ga, my=m) for m in XS}
    s_x = {(0, m): send(sk_hbm, own_gs, mx=m) for m in XS}

    def forward_z(m):
        s_z[m].wait_recv()
        ref = gs.at[gs_at(flip(zl, m), x)]
        for mx in XS:
            s_x[m, mx] = send(ref, ref, mx=mx)

    for m in (1, 2, 3):
        forward_z(m)
    a_zh.wait_recv()
    ref = ga.at[ga_at(y, flip(zh, 1), co)]
    for m in XS:
        a_y[m, 1] = send(ref, ref, my=m)
    own_ad.wait()
    ref = ga.at[ga_at(y, 0, co, 4)]
    a_co = {0: send(ref, ref, mco=1)}
    forward_z(4)
    forward_z(5)
    for m in XS:
        a_y[m, 0].wait_recv()
        a_y[m, 1].wait_recv()
        ref = ga.at[ga_at(flip(y, m), 0, co, 4)]
        a_co[m] = send(ref, ref, mco=1)
    forward_z(6)
    forward_z(7)
    for cp in loads:
        cp.wait()
    for m in (0,) + XS:
        a_co[m].wait_recv()

    def backward(k, carry):
        g = ga[tab[T_ROW + k]]
        prod = lax.dot_general(g, w[k], (((1,), (0,)), ((), ())), preferred_element_type=jnp.float32)
        accc[k + 1] = prod + accc[tab[T_PREVC + k]]
        return carry

    lax.fori_loop(0, SLOTS, backward, 0, unroll=8)

    def part_c(zl_, x_, s):
        return accc[tab[T_LASTC + (zl_ * 4 + x_) * 2 + s]]

    r_x = {}
    for mz in Z_FAR + (0,):
        for mx in XS:
            for s in range(2):
                sx[mx, mz, s] = part_c(flip(zl, mz), flip(x, mx), s)
            r_x[mx, mz] = send(sx.at[mx, mz], rx.at[mx, mz], mx=mx)

    own_sk.wait()
    for m in (0,) + Z_NEAR:
        for mx in XS:
            s_x[m, mx].wait_recv()

    def forward(k, carry):
        g = gs[tab[T_COL + k]]
        prod = lax.dot_general(g, w[k], (((1,), (1,)), ((), ())), preferred_element_type=jnp.float32)
        accr[k + 1] = prod + accr[tab[T_PREVR + k]]
        return carry

    r_z = {}

    def sum_x(mz, s):
        tot = part_c(flip(zl, mz), x, s)
        for mx in XS:
            tot = tot + rx[mx, mz, s]
        return tot

    def col_step(mz):
        for mx in XS:
            r_x[mx, mz].wait_recv()
        if mz:
            for s in range(2):
                sz[mz, s] = sum_x(mz, s)
            r_z[mz] = send(sz.at[mz], rz.at[mz], mz=mz)

    lax.fori_loop(0, SLOTS // 2, forward, 0, unroll=8)
    col_step(7)
    lax.fori_loop(SLOTS // 2, SLOTS, forward, 0, unroll=8)

    def part_r(y_, zh_, co_, s):
        return accr[tab[T_LASTR + (y_ * 4 + zh_ * 2 + co_) * 2 + s]]

    r_c = {}
    for m in XS + (0,):
        for h in range(2):
            for s in range(2):
                sc[m, h * 2 + s] = part_r(flip(y, m), flip(zh, h), flip(co, 1), s)
        r_c[m] = send(sc.at[m], rc.at[m], mco=1)
    col_step(6)
    r_y = {}
    for m in XS:
        r_c[m].wait_recv()
        for h in range(2):
            for s in range(2):
                sy[m, h * 2 + s] = part_r(flip(y, m), flip(zh, h), co, s) + rc[m, h * 2 + s]
        r_y[m] = send(sy.at[m], ry.at[m], my=m)
    col_step(5)
    col_step(4)
    r_c[0].wait_recv()
    for m in XS:
        r_y[m].wait_recv()

    def sum_y(h, s):
        tot = part_r(y, flip(zh, h), co, s) + rc[0, h * 2 + s]
        for m in XS:
            tot = tot + ry[m, h * 2 + s]
        return tot

    for s in range(2):
        sh[s] = sum_y(1, s)
    r_h = send(sh, rh, mzh=1)
    for mz in (3, 2, 1, 0):
        col_step(mz)
    r_h.wait_recv()
    for s in range(2):
        img_ref[s] = sum_y(0, s) + rh[s]
    for m in Z_NEAR:
        r_z[m].wait_recv()
    for s in range(2):
        tot = sum_x(0, s)
        for m in Z_NEAR:
            tot = tot + rz[m, s]
        coi_ref[s] = tot
    for cp in sent:
        cp.wait_send()


def table(rows_k, cols_k, count):
    slot = jnp.arange(SLOTS, dtype=jnp.int32)
    ends = jnp.arange(NC, dtype=jnp.int32)
    keys = jnp.stack([rows_k, cols_k])
    query = jnp.stack([jnp.concatenate([rows_k, ends]), jnp.concatenate([cols_k, ends])])
    limit = jnp.concatenate([slot, jnp.broadcast_to(count, (NC,))])
    hit = (keys[:, None, :] == query[:, :, None]) & (slot[None, None, :] < limit[None, :, None])
    last = jnp.max(jnp.where(hit, slot + 1, 0), axis=-1)
    s, q = rows_k % 2, rows_k // 2
    where_row = ((q % 2) * 8 + (q // 4) * 2 + (q // 2) % 2) * 2 + s
    return jnp.concatenate([where_row, cols_k, last[0, :SLOTS], last[1, :SLOTS], last[0, SLOTS:], last[1, SLOTS:]])


def local(blocks, block_rows, block_cols, counts, sketch, adjoint_sketch):
    tab = table(block_rows[0, 0], block_cols[0, 0], counts[0, 0])
    f32, bf16 = jnp.float32, jnp.bfloat16
    blk = (COLS, BLK)
    out = jax.ShapeDtypeStruct((2,) + blk, f32)
    return pl.pallas_call(
        kernel,
        out_shape=(out, out),
        in_specs=[
            pl.BlockSpec(memory_space=pltpu.SMEM),
            pl.BlockSpec(memory_space=pl.ANY),
            pl.BlockSpec(memory_space=pl.ANY),
            pl.BlockSpec(memory_space=pl.ANY),
        ],
        out_specs=(pl.BlockSpec(memory_space=pltpu.VMEM), pl.BlockSpec(memory_space=pltpu.VMEM)),
        scratch_shapes=[
            pltpu.VMEM((SLOTS, BLK, BLK), bf16),
            pltpu.VMEM((NR,) + blk, bf16),
            pltpu.VMEM((NC,) + blk, bf16),
            pltpu.VMEM((SLOTS + 1,) + blk, f32),
            pltpu.VMEM((SLOTS + 1,) + blk, f32),
            pltpu.VMEM((4, 8, 2) + blk, f32),
            pltpu.VMEM((4, 8, 2) + blk, f32),
            pltpu.VMEM((8, 2) + blk, f32),
            pltpu.VMEM((8, 2) + blk, f32),
            pltpu.VMEM((4, 4) + blk, f32),
            pltpu.VMEM((4, 4) + blk, f32),
            pltpu.VMEM((4, 4) + blk, f32),
            pltpu.VMEM((4, 4) + blk, f32),
            pltpu.VMEM((2,) + blk, f32),
            pltpu.VMEM((2,) + blk, f32),
            pltpu.SemaphoreType.DMA((2,)),
            pltpu.SemaphoreType.DMA((4,)),
            pltpu.SemaphoreType.DMA((NSEM,)),
            pltpu.SemaphoreType.DMA((NSEM,)),
        ],
        compiler_params=pltpu.CompilerParams(
            collective_id=0, has_side_effects=True, vmem_limit_bytes=48 * 1024 * 1024),
        cost_estimate=pl.CostEstimate(flops=2 * 201326592 * 2, bytes_accessed=4400000, transcendentals=0),
        name="flow",
    )(tab, blocks, sketch, adjoint_sketch)


def solution(mesh):
    in_specs = (
        P("row", "col", None, None, None),
        P("row", "col", None),
        P("row", "col", None),
        P("row", "col"),
        P(("row", "col"), None, None),
        P(("col", "row"), None, None),
    )
    out_specs = (P(("col", "row"), None, None), P(("row", "col"), None, None))
    return jax.shard_map(local, mesh=mesh, in_specs=in_specs, out_specs=out_specs, check_vma=False)
```

```python
import jax
import jax.numpy as jnp
from jax import lax
from jax.experimental import pallas as pl
from jax.experimental.pallas import tpu as pltpu
from jax.sharding import PartitionSpec as P

SLOTS = 128
COLS = 48
BLK = 128
NR = 32
NC = 64
PREVR, PREVC, LASTR, LASTC = 0, 1, 2, 3
OTHERS = (1, 3, 2)
NSEM = 64
FULL = 32752.0
CODED2 = 2 * COLS + 16
CODED4 = 4 * COLS + 16


def encode(dst, vals):
    n = len(vals)
    row = lax.broadcasted_iota(jnp.int32, (16, BLK), 0)
    powers = jnp.zeros((16, BLK), jnp.int32)
    for i, v in enumerate(vals):
        most = jnp.maximum(jnp.max(jnp.abs(v), axis=0, keepdims=True), 1e-30)
        e = jnp.ceil(jnp.log2(most))
        whole = jnp.round(v * (jnp.exp2(-e) * FULL))
        dst[pl.ds(i * COLS, COLS)] = whole.astype(jnp.int32).astype(jnp.int16)
        powers = jnp.where(row == i, e.astype(jnp.int32), powers)
    dst[pl.ds(n * COLS, 16)] = powers.astype(jnp.int16)


def decode(src, n):
    powers = src[pl.ds(n * COLS, 16)].astype(jnp.int32).astype(jnp.float32)
    scale = jnp.exp2(powers) * (1.0 / FULL)
    return [src[pl.ds(i * COLS, COLS)].astype(jnp.int32).astype(jnp.float32) * scale[i:i + 1]
            for i in range(n)]


def flip(v, m):
    out = 0
    for bit in (1, 2, 4):
        b = (v // bit) % 2
        out = out + bit * ((1 - b) if (m & bit) else b)
    return out


def kernel(cnt, rows_hbm, cols_hbm, blk_hbm, sk_hbm, ad_hbm, out_ref,
           w, ga, gs, accr, accc, rows_s, cols_s, keys, wide, tabv, tab,
           sx, rx, sz, rz, sz2, rz2, sc, rc, sy, ry, sh, rh,
           lsem, wsem, ssem, rsem):
    r = lax.axis_index("row")
    c = lax.axis_index("col")
    y, zh, co = r // 4, (r // 2) % 2, r % 2
    zl, x = c // 4, c % 4

    def peer(my=0, mzh=0, mco=0, mz=0, mx=0):
        y2, zh2, co2 = flip(y, my), flip(zh, mzh), flip(co, mco)
        zl2, x2 = flip(zl, mz), flip(x, mx)
        return (y2 * 4 + zh2 * 2 + co2, zl2 * 4 + x2)

    peers = ([dict(mzh=1), dict(mz=4)] + [dict(mz=m) for m in OTHERS]
             + [dict(mx=m) for m in OTHERS] + [dict(my=m) for m in OTHERS] + [dict(mco=1)])
    bar = pltpu.get_barrier_semaphore()
    for p in peers:
        pl.semaphore_signal(bar, inc=1, device_id=peer(**p), device_id_type=pl.DeviceIdType.MESH)

    def ga_at(y_, zh_, co_, n=2):
        return pl.ds((co_ * 8 + y_ * 2 + zh_) * 2, n)

    def gs_at(zl_, x_, n=2):
        return pl.ds((x_ * 8 + zl_) * 2, n)

    def local_copy(src, dst, sem):
        cp = pltpu.make_async_copy(src, dst, sem)
        cp.start()
        return cp

    ids = [local_copy(rows_hbm, rows_s, lsem.at[2]),
           local_copy(cols_hbm, cols_s, lsem.at[3]),
           local_copy(rows_hbm, keys.at[0], lsem.at[4]),
           local_copy(cols_hbm, keys.at[1], lsem.at[5])]
    own_ad = local_copy(ad_hbm, ga.at[ga_at(y, zh, co)], lsem.at[0])
    own_sk = local_copy(sk_hbm, gs.at[gs_at(zl, x)], lsem.at[1])
    parts = 4
    loads = []
    for i in range(parts):
        n = SLOTS // parts
        loads.append(local_copy(blk_hbm.at[0, 0, pl.ds(i * n, n)], w.at[pl.ds(i * n, n)], wsem.at[i]))
    accr[0] = jnp.zeros((COLS, BLK), jnp.float32)
    accc[0] = jnp.zeros((COLS, BLK), jnp.float32)

    for cp in ids:
        cp.wait()

    def spread(j, carry):
        wide[0, pl.ds(j, 1)] = jnp.full((1, SLOTS), rows_s[0, j], jnp.int32)
        wide[1, pl.ds(j, 1)] = jnp.full((1, SLOTS), cols_s[0, j], jnp.int32)
        return carry

    lax.fori_loop(0, SLOTS, spread, 0, unroll=8)
    down = lax.broadcasted_iota(jnp.int32, (SLOTS, SLOTS), 0)
    across = lax.broadcasted_iota(jnp.int32, (SLOTS, SLOTS), 1)
    for i in range(2):
        same = (wide[i] == keys[i]) & (down < across)
        tabv[pl.ds(PREVR + i, 1)] = jnp.max(jnp.where(same, down + 1, 0), axis=0, keepdims=True)
        ends = (wide[i] == across) & (down < cnt[0, 0])
        tabv[pl.ds(LASTR + i, 1)] = jnp.max(jnp.where(ends, down + 1, 0), axis=0, keepdims=True)
    tab_copy = local_copy(tabv, tab, lsem.at[6])

    pl.semaphore_wait(bar, len(peers))

    count = [0]
    sent = []

    def send(src, dst, **p):
        i = count[0]
        count[0] += 1
        cp = pltpu.make_async_remote_copy(
            src_ref=src, dst_ref=dst, send_sem=ssem.at[i], recv_sem=rsem.at[i],
            device_id=peer(**p), device_id_type=pl.DeviceIdType.MESH)
        cp.start()
        sent.append(cp)
        return cp

    own_ga, own_gs = ga.at[ga_at(y, zh, co)], gs.at[gs_at(zl, x)]
    a_zh = send(ad_hbm, own_ga, mzh=1)
    s_4 = send(sk_hbm, own_gs, mz=4)
    s_z = [send(sk_hbm, own_gs, mz=m) for m in (3, 2, 1)]
    a_y = {(m, 0): send(ad_hbm, own_ga, my=m) for m in OTHERS}
    own_sk.wait()
    for cp in s_z:
        cp.wait_recv()
    quad = gs.at[gs_at(zl // 4 * 4, x, 8)]
    s_x = [send(quad, quad, mx=m) for m in OTHERS]
    s_4.wait_recv()
    ref = gs.at[gs_at(flip(zl, 4), x)]
    s_z4 = [send(ref, ref, mz=m) for m in (3, 2, 1)]
    own_ad.wait()
    a_zh.wait_recv()
    ref = ga.at[ga_at(y, flip(zh, 1), co)]
    for m in OTHERS:
        a_y[m, 1] = send(ref, ref, my=m)
    ref = ga.at[ga_at(y, 0, co, 4)]
    a_co = [send(ref, ref, mco=1)]
    for cp in s_z4:
        cp.wait_recv()
    quad = gs.at[gs_at(flip(zl, 4) // 4 * 4, x, 8)]
    s_x += [send(quad, quad, mx=m) for m in OTHERS]
    for m in OTHERS:
        a_y[m, 0].wait_recv()
        a_y[m, 1].wait_recv()
        ref = ga.at[ga_at(flip(y, m), 0, co, 4)]
        a_co.append(send(ref, ref, mco=1))
    tab_copy.wait()
    for cp in loads:
        cp.wait()
    for cp in a_co:
        cp.wait_recv()

    def backward(k, carry):
        q = rows_s[0, k]
        g = ga[(q // 2 % 2) * 16 + (q // 8) * 4 + (q // 4 % 2) * 2 + q % 2]
        prod = lax.dot_general(g, w[k], (((1,), (0,)), ((), ())), preferred_element_type=jnp.float32)
        accc[k + 1] = prod + accc[tab[PREVC, k]]
        return carry

    lax.fori_loop(0, SLOTS, backward, 0, unroll=8)

    def part_c(zl_, x_, s):
        return accc[tab[LASTC, (zl_ * 4 + x_) * 2 + s]]

    def both(m):
        return [(flip(zl, m ^ far), s) for far in (0, 4) for s in range(2)]

    r_x = {}
    for m in (1, 2, 3, 0):
        for mx in OTHERS:
            encode(sx.at[mx, m], [part_c(z_, flip(x, mx), s) for z_, s in both(m)])
            r_x[mx, m] = send(sx.at[mx, m], rx.at[mx, m], mx=mx)

    for cp in s_x:
        cp.wait_recv()

    def forward(k, carry):
        q = cols_s[0, k]
        g = gs[(q // 2 % 4) * 16 + (q // 8) * 2 + q % 2]
        prod = lax.dot_general(g, w[k], (((1,), (1,)), ((), ())), preferred_element_type=jnp.float32)
        accr[k + 1] = prod + accr[tab[PREVR, k]]
        return carry

    lax.fori_loop(0, SLOTS, forward, 0, unroll=8)

    def part_r(y_, zh_, co_, s):
        return accr[tab[LASTR, (y_ * 4 + zh_ * 2 + co_) * 2 + s]]

    pairs = [(h, s) for h in range(2) for s in range(2)]
    r_c = {}
    for m in OTHERS + (0,):
        for i, (h, s) in enumerate(pairs):
            sc[m, i] = part_r(flip(y, m), flip(zh, h), flip(co, 1), s)
        r_c[m] = send(sc.at[m], rc.at[m], mco=1)

    def sum_x(m):
        tot = [part_c(z_, x, s) for z_, s in both(m)]
        for mx in OTHERS:
            r_x[mx, m].wait_recv()
            tot = [a + b for a, b in zip(tot, decode(rx.at[mx, m], 4))]
        return tot

    r_z = {}

    def col_step(m):
        encode(sz.at[m], sum_x(m))
        r_z[m] = send(sz.at[m], rz.at[m], mz=m)

    col_step(1)
    r_y = {}
    for m in OTHERS:
        r_c[m].wait_recv()
        encode(sy.at[m], [part_r(flip(y, m), flip(zh, h), co, s) + rc[m, i] for i, (h, s) in enumerate(pairs)])
        r_y[m] = send(sy.at[m], ry.at[m], my=m)
    col_step(2)
    r_c[0].wait_recv()
    tot = [part_r(y, flip(zh, h), co, s) + rc[0, i] for i, (h, s) in enumerate(pairs)]
    for m in OTHERS:
        r_y[m].wait_recv()
        tot = [a + b for a, b in zip(tot, decode(ry.at[m], 4))]
    encode(sh, tot[2:])
    r_h = send(sh, rh, mzh=1)
    for s in range(2):
        out_ref[s] = tot[s]
    col_step(3)
    tot = sum_x(0)
    for m in OTHERS:
        r_z[m].wait_recv()
        tot = [a + b for a, b in zip(tot, decode(rz.at[m], 4))]
    encode(sz2, tot[2:])
    r_z2 = send(sz2, rz2, mz=4)
    for s in range(2):
        out_ref[2 + s] = tot[s]
    r_h.wait_recv()
    for s, v in enumerate(decode(rh, 2)):
        out_ref[s] += v
    r_z2.wait_recv()
    for s, v in enumerate(decode(rz2, 2)):
        out_ref[2 + s] += v
    for cp in sent:
        cp.wait_send()


def local(blocks, block_rows, block_cols, counts, sketch, adjoint_sketch):
    f32, bf16, i16, i32 = jnp.float32, jnp.bfloat16, jnp.int16, jnp.int32
    blk = (COLS, BLK)
    hbm = pl.BlockSpec(memory_space=pltpu.HBM)
    out = pl.pallas_call(
        kernel,
        out_shape=jax.ShapeDtypeStruct((4,) + blk, f32),
        in_specs=[pl.BlockSpec(memory_space=pltpu.SMEM), hbm, hbm, hbm, hbm, hbm],
        out_specs=pl.BlockSpec(memory_space=pltpu.VMEM),
        scratch_shapes=[
            pltpu.VMEM((SLOTS, BLK, BLK), bf16),
            pltpu.VMEM((NR,) + blk, bf16),
            pltpu.VMEM((NC,) + blk, bf16),
            pltpu.VMEM((SLOTS + 1,) + blk, f32),
            pltpu.VMEM((SLOTS + 1,) + blk, f32),
            pltpu.SMEM((1, SLOTS), i32),
            pltpu.SMEM((1, SLOTS), i32),
            pltpu.VMEM((2, 1, SLOTS), i32),
            pltpu.VMEM((2, SLOTS, SLOTS), i32),
            pltpu.VMEM((8, SLOTS), i32),
            pltpu.SMEM((8, SLOTS), i32),
            pltpu.VMEM((4, 4, CODED4, BLK), i16),
            pltpu.VMEM((4, 4, CODED4, BLK), i16),
            pltpu.VMEM((4, CODED4, BLK), i16),
            pltpu.VMEM((4, CODED4, BLK), i16),
            pltpu.VMEM((CODED2, BLK), i16),
            pltpu.VMEM((CODED2, BLK), i16),
            pltpu.VMEM((4, 4) + blk, f32),
            pltpu.VMEM((4, 4) + blk, f32),
            pltpu.VMEM((4, CODED4, BLK), i16),
            pltpu.VMEM((4, CODED4, BLK), i16),
            pltpu.VMEM((CODED2, BLK), i16),
            pltpu.VMEM((CODED2, BLK), i16),
            pltpu.SemaphoreType.DMA((7,)),
            pltpu.SemaphoreType.DMA((4,)),
            pltpu.SemaphoreType.DMA((NSEM,)),
            pltpu.SemaphoreType.DMA((NSEM,)),
        ],
        compiler_params=pltpu.CompilerParams(
            collective_id=0, has_side_effects=True, vmem_limit_bytes=62 * 1024 * 1024),
        cost_estimate=pl.CostEstimate(flops=2 * 201326592 * 2, bytes_accessed=4400000, transcendentals=0),
        name="flow",
    )(counts, block_rows[0], block_cols[0], blocks, sketch, adjoint_sketch)
    return out[:2], out[2:]


def solution(mesh):
    in_specs = (
        P("row", "col", None, None, None),
        P("row", "col", None),
        P("row", "col", None),
        P("row", "col"),
        P(("row", "col"), None, None),
        P(("col", "row"), None, None),
    )
    out_specs = (P(("col", "row"), None, None), P(("row", "col"), None, None))
    return jax.shard_map(local, mesh=mesh, in_specs=in_specs, out_specs=out_specs, check_vma=False)
```

```python
import jax
import jax.numpy as jnp
from jax import lax
from jax.experimental import pallas as pl
from jax.experimental.pallas import tpu as pltpu
from jax.sharding import PartitionSpec as P

SLOTS = 128
COLS = 48
BLK = 128
NR = 32
NC = 64
PREVR, PREVC, LASTR, LASTC = 0, 1, 2, 3
OTHERS = (1, 3, 2)
NSEM = 64
FULL = 32752.0
CODED2 = 2 * COLS + 16
CODED4 = 4 * COLS + 16


def encode(dst, vals):
    n = len(vals)
    row = lax.broadcasted_iota(jnp.int32, (16, BLK), 0)
    powers = jnp.zeros((16, BLK), jnp.int32)
    for i, v in enumerate(vals):
        most = jnp.maximum(jnp.max(jnp.abs(v), axis=0, keepdims=True), 1e-30)
        e = jnp.ceil(jnp.log2(most))
        whole = jnp.round(v * (jnp.exp2(-e) * FULL))
        dst[pl.ds(i * COLS, COLS)] = whole.astype(jnp.int32).astype(jnp.int16)
        powers = jnp.where(row == i, e.astype(jnp.int32), powers)
    dst[pl.ds(n * COLS, 16)] = powers.astype(jnp.int16)


def decode(src, n):
    powers = src[pl.ds(n * COLS, 16)].astype(jnp.int32).astype(jnp.float32)
    scale = jnp.exp2(powers) * (1.0 / FULL)
    return [src[pl.ds(i * COLS, COLS)].astype(jnp.int32).astype(jnp.float32) * scale[i:i + 1]
            for i in range(n)]


def flip(v, m):
    out = 0
    for bit in (1, 2, 4):
        b = (v // bit) % 2
        out = out + bit * ((1 - b) if (m & bit) else b)
    return out


def kernel(cnt, rows_hbm, cols_hbm, blk_hbm, sk_hbm, ad_hbm, out_ref,
           w, ga, gs, accr, accc, rows_s, cols_s, keys, wide, tabv, tab,
           sx, rx, sz, rz, sz2, rz2, sc, rc, sy, ry, sh, rh,
           lsem, wsem, ssem, rsem):
    r = lax.axis_index("row")
    c = lax.axis_index("col")
    y, zh, co = r // 4, (r // 2) % 2, r % 2
    zl, x = c // 4, c % 4

    def peer(my=0, mzh=0, mco=0, mz=0, mx=0):
        y2, zh2, co2 = flip(y, my), flip(zh, mzh), flip(co, mco)
        zl2, x2 = flip(zl, mz), flip(x, mx)
        return (y2 * 4 + zh2 * 2 + co2, zl2 * 4 + x2)

    peers = ([dict(mzh=1), dict(mz=4)] + [dict(mz=m) for m in OTHERS]
             + [dict(mx=m) for m in OTHERS] + [dict(my=m) for m in OTHERS] + [dict(mco=1)])
    bar = pltpu.get_barrier_semaphore()
    for p in peers:
        pl.semaphore_signal(bar, inc=1, device_id=peer(**p), device_id_type=pl.DeviceIdType.MESH)

    def ga_at(y_, zh_, co_, n=2):
        return pl.ds((co_ * 8 + y_ * 2 + zh_) * 2, n)

    def gs_at(zl_, x_, n=2):
        return pl.ds((x_ * 8 + zl_) * 2, n)

    def local_copy(src, dst, sem):
        cp = pltpu.make_async_copy(src, dst, sem)
        cp.start()
        return cp

    own_ad = local_copy(ad_hbm, ga.at[ga_at(y, zh, co)], lsem.at[0])
    own_sk = local_copy(sk_hbm, gs.at[gs_at(zl, x)], lsem.at[1])
    ids = [local_copy(rows_hbm, rows_s, lsem.at[2]),
           local_copy(cols_hbm, cols_s, lsem.at[3]),
           local_copy(rows_hbm, keys.at[0], lsem.at[4]),
           local_copy(cols_hbm, keys.at[1], lsem.at[5])]
    parts = 4
    loads = []
    for i in range(parts):
        n = SLOTS // parts
        loads.append(local_copy(blk_hbm.at[0, 0, pl.ds(i * n, n)], w.at[pl.ds(i * n, n)], wsem.at[i]))
    accr[0] = jnp.zeros((COLS, BLK), jnp.float32)
    accc[0] = jnp.zeros((COLS, BLK), jnp.float32)

    own_ad.wait()
    own_sk.wait()
    pl.semaphore_wait(bar, len(peers))

    count = [0]
    sent = []

    def send(src, dst, **p):
        i = count[0]
        count[0] += 1
        cp = pltpu.make_async_remote_copy(
            src_ref=src, dst_ref=dst, send_sem=ssem.at[i], recv_sem=rsem.at[i],
            device_id=peer(**p), device_id_type=pl.DeviceIdType.MESH)
        cp.start()
        sent.append(cp)
        return cp

    own_ga, own_gs = ga.at[ga_at(y, zh, co)], gs.at[gs_at(zl, x)]
    a_zh = send(own_ga, own_ga, mzh=1)
    s_4 = send(own_gs, own_gs, mz=4)
    s_z = [send(own_gs, own_gs, mz=m) for m in (3, 2, 1)]
    a_y = {(m, 0): send(own_ga, own_ga, my=m) for m in OTHERS}
    for cp in ids:
        cp.wait()

    def spread(j, carry):
        wide[0, pl.ds(j, 1)] = jnp.full((1, SLOTS), rows_s[0, j], jnp.int32)
        wide[1, pl.ds(j, 1)] = jnp.full((1, SLOTS), cols_s[0, j], jnp.int32)
        return carry

    lax.fori_loop(0, SLOTS, spread, 0, unroll=8)
    down = lax.broadcasted_iota(jnp.int32, (SLOTS, SLOTS), 0)
    across = lax.broadcasted_iota(jnp.int32, (SLOTS, SLOTS), 1)
    for i in range(2):
        same = (wide[i] == keys[i]) & (down < across)
        tabv[pl.ds(PREVR + i, 1)] = jnp.max(jnp.where(same, down + 1, 0), axis=0, keepdims=True)
        ends = (wide[i] == across) & (down < cnt[0, 0])
        tabv[pl.ds(LASTR + i, 1)] = jnp.max(jnp.where(ends, down + 1, 0), axis=0, keepdims=True)
    tab_copy = local_copy(tabv, tab, lsem.at[6])

    for cp in s_z:
        cp.wait_recv()
    quad = gs.at[gs_at(zl // 4 * 4, x, 8)]
    s_x = [send(quad, quad, mx=m) for m in OTHERS]
    s_4.wait_recv()
    ref = gs.at[gs_at(flip(zl, 4), x)]
    s_z4 = [send(ref, ref, mz=m) for m in (3, 2, 1)]
    a_zh.wait_recv()
    ref = ga.at[ga_at(y, flip(zh, 1), co)]
    for m in OTHERS:
        a_y[m, 1] = send(ref, ref, my=m)
    ref = ga.at[ga_at(y, 0, co, 4)]
    a_co = [send(ref, ref, mco=1)]
    for cp in s_z4:
        cp.wait_recv()
    quad = gs.at[gs_at(flip(zl, 4) // 4 * 4, x, 8)]
    s_x += [send(quad, quad, mx=m) for m in OTHERS]
    for m in OTHERS:
        a_y[m, 0].wait_recv()
        a_y[m, 1].wait_recv()
        ref = ga.at[ga_at(flip(y, m), 0, co, 4)]
        a_co.append(send(ref, ref, mco=1))
    tab_copy.wait()
    for cp in loads:
        cp.wait()
    for cp in a_co:
        cp.wait_recv()

    def product(panels, first, second, k, axis):
        both = lax.dot_general(
            jnp.concatenate([panels[first], panels[second]], axis=0),
            jnp.concatenate([w[k], w[k + 1]], axis=1 - axis),
            (((1,), (axis,)), ((), ())), preferred_element_type=jnp.float32)
        return both[:COLS, :BLK], both[COLS:, BLK:]

    def ga_of(k):
        q = rows_s[0, k]
        return (q // 2 % 2) * 16 + (q // 8) * 4 + (q // 4 % 2) * 2 + q % 2

    def backward(i, carry):
        k = 2 * i
        one, two = product(ga, ga_of(k), ga_of(k + 1), k, 0)
        accc[k + 1] = one + accc[tab[PREVC, k]]
        accc[k + 2] = two + accc[tab[PREVC, k + 1]]
        return carry

    lax.fori_loop(0, SLOTS // 2, backward, 0, unroll=16)

    def part_c(zl_, x_, s):
        return accc[tab[LASTC, (zl_ * 4 + x_) * 2 + s]]

    def both(m):
        return [(flip(zl, m ^ far), s) for far in (0, 4) for s in range(2)]

    r_x = {}
    for m in (1, 2, 3, 0):
        for mx in OTHERS:
            encode(sx.at[mx, m], [part_c(z_, flip(x, mx), s) for z_, s in both(m)])
            r_x[mx, m] = send(sx.at[mx, m], rx.at[mx, m], mx=mx)

    for cp in s_x:
        cp.wait_recv()

    def gs_of(k):
        q = cols_s[0, k]
        return (q // 2 % 4) * 16 + (q // 8) * 2 + q % 2

    def forward(i, carry):
        k = 2 * i
        one, two = product(gs, gs_of(k), gs_of(k + 1), k, 1)
        accr[k + 1] = one + accr[tab[PREVR, k]]
        accr[k + 2] = two + accr[tab[PREVR, k + 1]]
        return carry

    lax.fori_loop(0, SLOTS // 2, forward, 0, unroll=16)

    def part_r(y_, zh_, co_, s):
        return accr[tab[LASTR, (y_ * 4 + zh_ * 2 + co_) * 2 + s]]

    pairs = [(h, s) for h in range(2) for s in range(2)]
    r_c = {}
    for m in OTHERS + (0,):
        for i, (h, s) in enumerate(pairs):
            sc[m, i] = part_r(flip(y, m), flip(zh, h), flip(co, 1), s)
        r_c[m] = send(sc.at[m], rc.at[m], mco=1)

    def sum_x(m):
        tot = [part_c(z_, x, s) for z_, s in both(m)]
        for mx in OTHERS:
            r_x[mx, m].wait_recv()
            tot = [a + b for a, b in zip(tot, decode(rx.at[mx, m], 4))]
        return tot

    r_z = {}

    def col_step(m):
        encode(sz.at[m], sum_x(m))
        r_z[m] = send(sz.at[m], rz.at[m], mz=m)

    col_step(1)
    r_y = {}
    for m in OTHERS:
        r_c[m].wait_recv()
        encode(sy.at[m], [part_r(flip(y, m), flip(zh, h), co, s) + rc[m, i] for i, (h, s) in enumerate(pairs)])
        r_y[m] = send(sy.at[m], ry.at[m], my=m)
    col_step(2)
    r_c[0].wait_recv()
    tot = [part_r(y, flip(zh, h), co, s) + rc[0, i] for i, (h, s) in enumerate(pairs)]
    for m in OTHERS:
        r_y[m].wait_recv()
        tot = [a + b for a, b in zip(tot, decode(ry.at[m], 4))]
    encode(sh, tot[2:])
    r_h = send(sh, rh, mzh=1)
    for s in range(2):
        out_ref[s] = tot[s]
    col_step(3)
    tot = sum_x(0)
    for m in OTHERS:
        r_z[m].wait_recv()
        tot = [a + b for a, b in zip(tot, decode(rz.at[m], 4))]
    encode(sz2, tot[2:])
    r_z2 = send(sz2, rz2, mz=4)
    for s in range(2):
        out_ref[2 + s] = tot[s]
    r_h.wait_recv()
    for s, v in enumerate(decode(rh, 2)):
        out_ref[s] += v
    r_z2.wait_recv()
    for s, v in enumerate(decode(rz2, 2)):
        out_ref[2 + s] += v
    for cp in sent:
        cp.wait_send()


def local(blocks, block_rows, block_cols, counts, sketch, adjoint_sketch):
    f32, bf16, i16, i32 = jnp.float32, jnp.bfloat16, jnp.int16, jnp.int32
    blk = (COLS, BLK)
    hbm = pl.BlockSpec(memory_space=pltpu.HBM)
    out = pl.pallas_call(
        kernel,
        out_shape=jax.ShapeDtypeStruct((4,) + blk, f32),
        in_specs=[pl.BlockSpec(memory_space=pltpu.SMEM), hbm, hbm, hbm, hbm, hbm],
        out_specs=pl.BlockSpec(memory_space=pltpu.VMEM),
        scratch_shapes=[
            pltpu.VMEM((SLOTS, BLK, BLK), bf16),
            pltpu.VMEM((NR,) + blk, bf16),
            pltpu.VMEM((NC,) + blk, bf16),
            pltpu.VMEM((SLOTS + 1,) + blk, f32),
            pltpu.VMEM((SLOTS + 1,) + blk, f32),
            pltpu.SMEM((1, SLOTS), i32),
            pltpu.SMEM((1, SLOTS), i32),
            pltpu.VMEM((2, 1, SLOTS), i32),
            pltpu.VMEM((2, SLOTS, SLOTS), i32),
            pltpu.VMEM((8, SLOTS), i32),
            pltpu.SMEM((8, SLOTS), i32),
            pltpu.VMEM((4, 4, CODED4, BLK), i16),
            pltpu.VMEM((4, 4, CODED4, BLK), i16),
            pltpu.VMEM((4, CODED4, BLK), i16),
            pltpu.VMEM((4, CODED4, BLK), i16),
            pltpu.VMEM((CODED2, BLK), i16),
            pltpu.VMEM((CODED2, BLK), i16),
            pltpu.VMEM((4, 4) + blk, f32),
            pltpu.VMEM((4, 4) + blk, f32),
            pltpu.VMEM((4, CODED4, BLK), i16),
            pltpu.VMEM((4, CODED4, BLK), i16),
            pltpu.VMEM((CODED2, BLK), i16),
            pltpu.VMEM((CODED2, BLK), i16),
            pltpu.SemaphoreType.DMA((7,)),
            pltpu.SemaphoreType.DMA((4,)),
            pltpu.SemaphoreType.DMA((NSEM,)),
            pltpu.SemaphoreType.DMA((NSEM,)),
        ],
        compiler_params=pltpu.CompilerParams(
            collective_id=0, has_side_effects=True, vmem_limit_bytes=62 * 1024 * 1024),
        cost_estimate=pl.CostEstimate(flops=2 * 201326592 * 2, bytes_accessed=4400000, transcendentals=0),
        name="flow",
    )(counts, block_rows[0], block_cols[0], blocks, sketch, adjoint_sketch)
    return out[:2], out[2:]


def solution(mesh):
    in_specs = (
        P("row", "col", None, None, None),
        P("row", "col", None),
        P("row", "col", None),
        P("row", "col"),
        P(("row", "col"), None, None),
        P(("col", "row"), None, None),
    )
    out_specs = (P(("col", "row"), None, None), P(("row", "col"), None, None))
    return jax.shard_map(local, mesh=mesh, in_specs=in_specs, out_specs=out_specs, check_vma=False)
```

```python
import jax
import jax.numpy as jnp
from jax import lax
from jax.experimental import pallas as pl
from jax.experimental.pallas import tpu as pltpu
from jax.sharding import PartitionSpec as P

SLOTS = 128
COLS = 48
BLK = 128
NR = 32
NC = 64
PREVR, PREVC, LASTR, LASTC = 0, 1, 2, 3
OTHERS = (1, 3, 2)
NSEM = 64
FULL = 32752.0
CODED2 = 2 * COLS + 16
CODED4 = 4 * COLS + 16


def encode(dst, vals):
    n = len(vals)
    row = lax.broadcasted_iota(jnp.int32, (16, BLK), 0)
    powers = jnp.zeros((16, BLK), jnp.int32)
    for i, v in enumerate(vals):
        most = jnp.maximum(jnp.max(jnp.abs(v), axis=0, keepdims=True), 1e-30)
        e = jnp.ceil(jnp.log2(most))
        whole = jnp.round(v * (jnp.exp2(-e) * FULL))
        dst[pl.ds(i * COLS, COLS)] = whole.astype(jnp.int32).astype(jnp.int16)
        powers = jnp.where(row == i, e.astype(jnp.int32), powers)
    dst[pl.ds(n * COLS, 16)] = powers.astype(jnp.int16)


def decode(src, n):
    powers = src[pl.ds(n * COLS, 16)].astype(jnp.int32).astype(jnp.float32)
    scale = jnp.exp2(powers) * (1.0 / FULL)
    return [src[pl.ds(i * COLS, COLS)].astype(jnp.int32).astype(jnp.float32) * scale[i:i + 1]
            for i in range(n)]


def flip(v, m):
    out = 0
    for bit in (1, 2, 4):
        b = (v // bit) % 2
        out = out + bit * ((1 - b) if (m & bit) else b)
    return out


def kernel(cnt, rows_hbm, cols_hbm, blk_hbm, sk_hbm, ad_hbm, out_ref,
           w, ga, gs, accr, accc, rows_s, cols_s, keys, wide, tabv, tab,
           sx, rx, sz, rz, sz2, rz2, sc, rc, sy, ry, sh, rh,
           lsem, wsem, ssem, rsem):
    r = lax.axis_index("row")
    c = lax.axis_index("col")
    y, zh, co = r // 4, (r // 2) % 2, r % 2
    zl, x = c // 4, c % 4

    def peer(my=0, mzh=0, mco=0, mz=0, mx=0):
        y2, zh2, co2 = flip(y, my), flip(zh, mzh), flip(co, mco)
        zl2, x2 = flip(zl, mz), flip(x, mx)
        return (y2 * 4 + zh2 * 2 + co2, zl2 * 4 + x2)

    peers = ([dict(mzh=1), dict(mz=4)] + [dict(mz=m) for m in OTHERS]
             + [dict(mx=m) for m in OTHERS] + [dict(my=m) for m in OTHERS] + [dict(mco=1)])
    bar = pltpu.get_barrier_semaphore()
    for p in peers:
        pl.semaphore_signal(bar, inc=1, device_id=peer(**p), device_id_type=pl.DeviceIdType.MESH)

    def ga_at(y_, zh_, co_, n=2):
        return pl.ds((co_ * 8 + y_ * 2 + zh_) * 2, n)

    def gs_at(zl_, x_, n=2):
        return pl.ds((x_ * 8 + zl_) * 2, n)

    def local_copy(src, dst, sem):
        cp = pltpu.make_async_copy(src, dst, sem)
        cp.start()
        return cp

    own_ad = local_copy(ad_hbm, ga.at[ga_at(y, zh, co)], lsem.at[0])
    own_sk = local_copy(sk_hbm, gs.at[gs_at(zl, x)], lsem.at[1])
    ids = [local_copy(rows_hbm, rows_s, lsem.at[2]),
           local_copy(cols_hbm, cols_s, lsem.at[3]),
           local_copy(rows_hbm, keys.at[0], lsem.at[4]),
           local_copy(cols_hbm, keys.at[1], lsem.at[5])]
    parts = 4
    loads = []
    for i in range(parts):
        n = SLOTS // parts
        loads.append(local_copy(blk_hbm.at[0, 0, pl.ds(i * n, n)], w.at[pl.ds(i * n, n)], wsem.at[i]))
    accr[0] = jnp.zeros((COLS, BLK), jnp.float32)
    accc[0] = jnp.zeros((COLS, BLK), jnp.float32)

    own_ad.wait()
    own_sk.wait()
    pl.semaphore_wait(bar, len(peers))

    count = [0]
    sent = []

    def send(src, dst, **p):
        i = count[0]
        count[0] += 1
        cp = pltpu.make_async_remote_copy(
            src_ref=src, dst_ref=dst, send_sem=ssem.at[i], recv_sem=rsem.at[i],
            device_id=peer(**p), device_id_type=pl.DeviceIdType.MESH)
        cp.start()
        sent.append(cp)
        return cp

    own_ga, own_gs = ga.at[ga_at(y, zh, co)], gs.at[gs_at(zl, x)]
    a_zh = send(own_ga, own_ga, mzh=1)
    s_4 = send(own_gs, own_gs, mz=4)
    s_z = [send(own_gs, own_gs, mz=m) for m in (3, 2, 1)]
    a_y = {(m, 0): send(own_ga, own_ga, my=m) for m in OTHERS}
    for cp in ids:
        cp.wait()

    def spread(j, carry):
        wide[0, pl.ds(j, 1)] = jnp.full((1, SLOTS), rows_s[0, j], jnp.int32)
        wide[1, pl.ds(j, 1)] = jnp.full((1, SLOTS), cols_s[0, j], jnp.int32)
        return carry

    lax.fori_loop(0, SLOTS, spread, 0, unroll=8)
    down = lax.broadcasted_iota(jnp.int32, (SLOTS, SLOTS), 0)
    across = lax.broadcasted_iota(jnp.int32, (SLOTS, SLOTS), 1)
    for i in range(2):
        same = (wide[i] == keys[i]) & (down < across)
        tabv[pl.ds(PREVR + i, 1)] = jnp.max(jnp.where(same, down + 1, 0), axis=0, keepdims=True)
        ends = (wide[i] == across) & (down < cnt[0, 0])
        tabv[pl.ds(LASTR + i, 1)] = jnp.max(jnp.where(ends, down + 1, 0), axis=0, keepdims=True)
    tab_copy = local_copy(tabv, tab, lsem.at[6])

    for cp in s_z:
        cp.wait_recv()
    quad = gs.at[gs_at(zl // 4 * 4, x, 8)]
    s_x = [send(quad, quad, mx=m) for m in OTHERS]
    s_4.wait_recv()
    ref = gs.at[gs_at(flip(zl, 4), x)]
    s_z4 = [send(ref, ref, mz=m) for m in (3, 2, 1)]
    a_zh.wait_recv()
    ref = ga.at[ga_at(y, flip(zh, 1), co)]
    for m in OTHERS:
        a_y[m, 1] = send(ref, ref, my=m)
    ref = ga.at[ga_at(y, 0, co, 4)]
    a_co = [send(ref, ref, mco=1)]
    for cp in s_z4:
        cp.wait_recv()
    quad = gs.at[gs_at(flip(zl, 4) // 4 * 4, x, 8)]
    s_x += [send(quad, quad, mx=m) for m in OTHERS]
    for m in OTHERS:
        a_y[m, 0].wait_recv()
        a_y[m, 1].wait_recv()
        ref = ga.at[ga_at(flip(y, m), 0, co, 4)]
        a_co.append(send(ref, ref, mco=1))
    tab_copy.wait()
    for cp in loads:
        cp.wait()
    for cp in a_co:
        cp.wait_recv()

    def product(panels, first, second, k, axis):
        both = lax.dot_general(
            jnp.concatenate([panels[first], panels[second]], axis=0),
            jnp.concatenate([w[k], w[k + 1]], axis=1 - axis),
            (((1,), (axis,)), ((), ())), preferred_element_type=jnp.float32)
        return both[:COLS, :BLK], both[COLS:, BLK:]

    def ga_of(k):
        q = rows_s[0, k]
        return (q // 2 % 2) * 16 + (q // 8) * 4 + (q // 4 % 2) * 2 + q % 2

    def backward(i, carry):
        k = 2 * i
        one, two = product(ga, ga_of(k), ga_of(k + 1), k, 0)
        accc[k + 1] = one + accc[tab[PREVC, k]]
        accc[k + 2] = two + accc[tab[PREVC, k + 1]]
        return carry

    lax.fori_loop(0, SLOTS // 2, backward, 0, unroll=16)

    def part_c(zl_, x_, s):
        return accc[tab[LASTC, (zl_ * 4 + x_) * 2 + s]]

    def both(m):
        return [(flip(zl, m ^ far), s) for far in (0, 4) for s in range(2)]

    r_x = {}
    for m in (1, 2, 3, 0):
        for mx in OTHERS:
            encode(sx.at[mx, m], [part_c(z_, flip(x, mx), s) for z_, s in both(m)])
            r_x[mx, m] = send(sx.at[mx, m], rx.at[mx, m], mx=mx)

    for cp in s_x:
        cp.wait_recv()

    def gs_of(k):
        q = cols_s[0, k]
        return (q // 2 % 4) * 16 + (q // 8) * 2 + q % 2

    def forward(i, carry):
        k = 2 * i
        one, two = product(gs, gs_of(k), gs_of(k + 1), k, 1)
        accr[k + 1] = one + accr[tab[PREVR, k]]
        accr[k + 2] = two + accr[tab[PREVR, k + 1]]
        return carry

    lax.fori_loop(0, SLOTS // 2, forward, 0, unroll=16)

    def part_r(y_, zh_, co_, s):
        return accr[tab[LASTR, (y_ * 4 + zh_ * 2 + co_) * 2 + s]]

    pairs = [(h, s) for h in range(2) for s in range(2)]
    r_c = {}
    for m in OTHERS + (0,):
        for i, (h, s) in enumerate(pairs):
            sc[m, i] = part_r(flip(y, m), flip(zh, h), flip(co, 1), s)
        r_c[m] = send(sc.at[m], rc.at[m], mco=1)

    def sum_x(m):
        tot = [part_c(z_, x, s) for z_, s in both(m)]
        for mx in OTHERS:
            r_x[mx, m].wait_recv()
            tot = [a + b for a, b in zip(tot, decode(rx.at[mx, m], 4))]
        return tot

    r_z = {}

    def col_step(m):
        encode(sz.at[m], sum_x(m))
        r_z[m] = send(sz.at[m], rz.at[m], mz=m)

    r_y = {}
    for m in OTHERS:
        r_c[m].wait_recv()
        encode(sy.at[m], [part_r(flip(y, m), flip(zh, h), co, s) + rc[m, i] for i, (h, s) in enumerate(pairs)])
        r_y[m] = send(sy.at[m], ry.at[m], my=m)
    col_step(1)
    col_step(2)
    r_c[0].wait_recv()
    tot = [part_r(y, flip(zh, h), co, s) + rc[0, i] for i, (h, s) in enumerate(pairs)]
    for m in OTHERS:
        r_y[m].wait_recv()
        tot = [a + b for a, b in zip(tot, decode(ry.at[m], 4))]
    encode(sh, tot[2:])
    r_h = send(sh, rh, mzh=1)
    for s in range(2):
        out_ref[s] = tot[s]
    col_step(3)
    tot = sum_x(0)
    for m in OTHERS:
        r_z[m].wait_recv()
        tot = [a + b for a, b in zip(tot, decode(rz.at[m], 4))]
    encode(sz2, tot[2:])
    r_z2 = send(sz2, rz2, mz=4)
    for s in range(2):
        out_ref[2 + s] = tot[s]
    r_h.wait_recv()
    for s, v in enumerate(decode(rh, 2)):
        out_ref[s] += v
    r_z2.wait_recv()
    for s, v in enumerate(decode(rz2, 2)):
        out_ref[2 + s] += v
    for cp in sent:
        cp.wait_send()


def local(blocks, block_rows, block_cols, counts, sketch, adjoint_sketch):
    f32, bf16, i16, i32 = jnp.float32, jnp.bfloat16, jnp.int16, jnp.int32
    blk = (COLS, BLK)
    hbm = pl.BlockSpec(memory_space=pltpu.HBM)
    out = pl.pallas_call(
        kernel,
        out_shape=jax.ShapeDtypeStruct((4,) + blk, f32),
        in_specs=[pl.BlockSpec(memory_space=pltpu.SMEM), hbm, hbm, hbm, hbm, hbm],
        out_specs=pl.BlockSpec(memory_space=pltpu.VMEM),
        scratch_shapes=[
            pltpu.VMEM((SLOTS, BLK, BLK), bf16),
            pltpu.VMEM((NR,) + blk, bf16),
            pltpu.VMEM((NC,) + blk, bf16),
            pltpu.VMEM((SLOTS + 1,) + blk, f32),
            pltpu.VMEM((SLOTS + 1,) + blk, f32),
            pltpu.SMEM((1, SLOTS), i32),
            pltpu.SMEM((1, SLOTS), i32),
            pltpu.VMEM((2, 1, SLOTS), i32),
            pltpu.VMEM((2, SLOTS, SLOTS), i32),
            pltpu.VMEM((8, SLOTS), i32),
            pltpu.SMEM((8, SLOTS), i32),
            pltpu.VMEM((4, 4, CODED4, BLK), i16),
            pltpu.VMEM((4, 4, CODED4, BLK), i16),
            pltpu.VMEM((4, CODED4, BLK), i16),
            pltpu.VMEM((4, CODED4, BLK), i16),
            pltpu.VMEM((CODED2, BLK), i16),
            pltpu.VMEM((CODED2, BLK), i16),
            pltpu.VMEM((4, 4) + blk, f32),
            pltpu.VMEM((4, 4) + blk, f32),
            pltpu.VMEM((4, CODED4, BLK), i16),
            pltpu.VMEM((4, CODED4, BLK), i16),
            pltpu.VMEM((CODED2, BLK), i16),
            pltpu.VMEM((CODED2, BLK), i16),
            pltpu.SemaphoreType.DMA((7,)),
            pltpu.SemaphoreType.DMA((4,)),
            pltpu.SemaphoreType.DMA((NSEM,)),
            pltpu.SemaphoreType.DMA((NSEM,)),
        ],
        compiler_params=pltpu.CompilerParams(
            collective_id=0, has_side_effects=True, vmem_limit_bytes=62 * 1024 * 1024),
        cost_estimate=pl.CostEstimate(flops=2 * 201326592 * 2, bytes_accessed=4400000, transcendentals=0),
        name="flow",
    )(counts, block_rows[0], block_cols[0], blocks, sketch, adjoint_sketch)
    return out[:2], out[2:]


def solution(mesh):
    in_specs = (
        P("row", "col", None, None, None),
        P("row", "col", None),
        P("row", "col", None),
        P("row", "col"),
        P(("row", "col"), None, None),
        P(("col", "row"), None, None),
    )
    out_specs = (P(("col", "row"), None, None), P(("row", "col"), None, None))
    return jax.shard_map(local, mesh=mesh, in_specs=in_specs, out_specs=out_specs, check_vma=False)
```
